512 devices in a mesh: seq: 32 (over z_hi, y, core), doc: 16 (over x, z_lo).
Axes of the slice: x: 4, y: 8, z: 8 (z_hi: 2, z_lo: 4; z = z_hi * 4 + z_lo), core: 2. Of those that a mesh axis runs over, the one named last changes fastest.
Arguments:
- self_q: bfloat16 [16, 4096, 4096], P('doc', 'seq'), may hold values from -5 to 5
- self_kv: bfloat16 [16, 4096, 2048], P('doc', 'seq'), may hold values from -5 to 5
- doc_ids: int32 [16, 4096], P('doc', 'seq'), may hold values from 0 to 7, never falling along the last dimension, each value on 1 to 1024 neighbouring positions
- cross_q: bfloat16 [16, 4096, 4096], P('doc', 'seq'), may hold values from -5 to 5
- vision_kv: bfloat16 [16, 32, 128, 2048], P(None, 'seq', 'doc'), may hold values from -5 to 5
- span_image: int32 [16, 64], P('doc'), may hold values from 0 to 31, as said below
- image_slot: int32 [16, 32], P('doc'), may hold values from 0 to 31, each once within a row
- cross_gate: float32 [1], replicated, may hold values from 0.5 to 1.5
Outputs:
- mixed: bfloat16 [16, 4096, 4096], P('doc', 'seq')
The draws below stay inside these ranges and needn't reach their ends.
Inputs may be any that keep to these rules, and one draw needn't show every extreme that they name: `span_image`: non-decreasing along each document; every image 0 to 31 is attended by at least one span.
All inputs are finite; a program needn't handle non-finite values.
Results may differ from the reference program's by a relative error of at most 0.0075.
Values may be sent and summed in bfloat16 or wider, within the bound.
No kernel may reach another device: no remote copies, remote signals or barrier semaphores. Data moves between devices by JAX's collectives and lax.ppermute only.
A program may use at most 64 MiB of HBM per device.

```python
import math
import jax
import jax.numpy as jnp
import numpy as np
from jax import lax

HEADS = 32
KV_HEADS = 8
HEAD_DIM = 128
V = 128
SPAN = 64
SEGS = 8
SEQLEN = 4096
DOCS = 16
IMGS = 32
SPANS = 64


def draw_self_q(key, part):
    key = jax.random.fold_in(key, 11)
    shape = (DOCS, SEQLEN, HEADS * HEAD_DIM)
    field = jnp.clip(jax.random.normal(key, shape, jnp.float32), -4.5, 4.5)
    return field.astype(jnp.bfloat16)


def draw_cross_q(key, part):
    key = jax.random.fold_in(key, 13)
    shape = (DOCS, SEQLEN, HEADS * HEAD_DIM)
    field = jnp.clip(jax.random.normal(key, shape, jnp.float32), -4.5, 4.5)
    return field.astype(jnp.bfloat16)


def draw_self_kv(key, part):
    key = jax.random.fold_in(key, 17)
    shape = (DOCS, SEQLEN, 2 * KV_HEADS * HEAD_DIM)
    field = jnp.clip(jax.random.normal(key, shape, jnp.float32), -4.5, 4.5)
    return field.astype(jnp.bfloat16)


def draw_vision_kv(key, part):
    key = jax.random.fold_in(key, 19)
    shape = (DOCS, IMGS, V, 2 * KV_HEADS * HEAD_DIM)
    field = jnp.clip(jax.random.normal(key, shape, jnp.float32), -4.5, 4.5)
    return field.astype(jnp.bfloat16)


def draw_span_image(key, part):
    key = jax.random.fold_in(key, 23)

    def one_row(row_key):
        order = jax.random.permutation(row_key, SPANS - 1)
        cuts = order[:IMGS - 1] + 1
        marks = jnp.zeros((SPANS,), jnp.int32).at[cuts].set(1)
        return jnp.cumsum(marks).astype(jnp.int32)
    return jax.vmap(one_row)(jax.random.split(key, DOCS))


def split_up(number_of, total, most, skew):
    loads = [(1 << 20) // math.isqrt(grade ** skew) + 1 for grade in range(2, number_of + 1)]
    surplus, counts = total - most - (number_of - 1), [1] * (number_of - 1)
    while surplus > 0:
        candidates = [i for i in range(number_of - 1) if counts[i] < most]
        pool, budget = sum([loads[i] for i in candidates]), surplus
        for i in candidates:
            extra = min(most - counts[i], max(1, budget * loads[i] // pool), surplus)
            counts[i] = counts[i] + extra
            surplus = surplus - extra
    return np.array([most] + counts)


def uneven(rng, count, total, reach, skew):
    if count == 2:
        one = jax.random.randint(rng, (), max(1, total - reach), min(reach, total - 1) + 1)
        return jnp.stack([one, total - one])
    tallies = jnp.asarray(split_up(count, total, reach, skew), jnp.int32)
    pairs = (count - 1) // 2
    source_of, receiver = tallies[1:1 + 2 * pairs:2], tallies[2:2 + 2 * pairs:2]
    margin = jnp.minimum(source_of - 1, reach - receiver)
    passed = jax.random.randint(jax.random.fold_in(rng, 1), (pairs,), 0, 1 << 20) % (margin + 1)
    tallies = tallies.at[1:1 + 2 * pairs:2].set(source_of - passed).at[2:2 + 2 * pairs:2].set(receiver + passed)
    return tallies[jax.random.permutation(jax.random.fold_in(rng, 2), count)]


def setup_inputs(seed: int = 0) -> dict:
    seeds = jax.random.split(jax.random.key(seed), 9)
    self_q = draw_self_q(jax.random.fold_in(seeds[8], 71), 0)
    self_kv = draw_self_kv(jax.random.fold_in(seeds[8], 71), 0)
    doc_ids = jax.vmap(lambda own: jnp.searchsorted(jnp.cumsum(uneven(own, SEGS, SEQLEN, SEQLEN // 4, 2)), jnp.arange(SEQLEN), side="right"))(jax.random.split(seeds[2], DOCS)).reshape((DOCS, SEQLEN)).astype(jnp.int32)
    cross_q = draw_cross_q(jax.random.fold_in(seeds[8], 71), 0)
    vision_kv = draw_vision_kv(jax.random.fold_in(seeds[8], 71), 0)
    span_image = draw_span_image(jax.random.fold_in(seeds[8], 71), 0)
    image_slot = jax.vmap(lambda own: jax.random.permutation(own, IMGS))(jax.random.split(seeds[6], DOCS)).reshape((DOCS, IMGS)).astype(jnp.int32)
    cross_gate = jnp.clip(jax.random.uniform(seeds[7], (1,), jnp.float32, 0.5, 1.5), 0.5, 1.5)
    return dict(self_q=self_q, self_kv=self_kv, doc_ids=doc_ids, cross_q=cross_q, vision_kv=vision_kv, span_image=span_image, image_slot=image_slot, cross_gate=cross_gate)


def reference(self_q, self_kv, doc_ids, cross_q, vision_kv, span_image, image_slot, cross_gate):
    groups = HEADS // KV_HEADS
    scale = HEAD_DIM ** -0.5
    gate = jnp.tanh(cross_gate[0])

    def one_doc(items):
        q_doc, kv_doc, ids, cq_doc, vis, spans, slots = items
        length = q_doc.shape[0]
        pos = jnp.arange(length, dtype=jnp.int32)
        visible = (pos[None, :] <= pos[:, None]) & (ids[None, :] == ids[:, None])
        q_heads = q_doc.reshape(length, HEADS, HEAD_DIM).transpose(1, 0, 2)
        kv_heads = kv_doc.reshape(length, 2, KV_HEADS, HEAD_DIM)
        k_heads = kv_heads[:, 0].transpose(1, 0, 2)
        v_heads = kv_heads[:, 1].transpose(1, 0, 2)
        chosen = slots[spans].astype(jnp.int32)
        cq_heads = cq_doc.reshape(SPANS, SPAN, HEADS, HEAD_DIM)
        vis_heads = vis.reshape(IMGS, V, 2, KV_HEADS, HEAD_DIM)

        def one_head(head):
            group = head // groups
            query = lax.dynamic_index_in_dim(q_heads, head, 0, keepdims=False)
            key = lax.dynamic_index_in_dim(k_heads, group, 0, keepdims=False)
            value = lax.dynamic_index_in_dim(v_heads, group, 0, keepdims=False)
            scores = jnp.dot(query, key.T, preferred_element_type=jnp.float32) * scale
            scores = jnp.where(visible, scores, -jnp.inf)
            top = jnp.max(scores, axis=1, keepdims=True)
            weights = jnp.where(visible, jnp.exp(scores - top), 0.0)
            total = jnp.sum(weights, axis=1, keepdims=True)
            self_ctx = (jnp.dot(weights.astype(jnp.bfloat16), value, preferred_element_type=jnp.float32) / total).astype(jnp.bfloat16)
            cquery = lax.dynamic_index_in_dim(cq_heads, head, 2, keepdims=False).astype(jnp.float32)
            ckey = lax.dynamic_index_in_dim(vis_heads[:, :, 0], group, 2, keepdims=False)[chosen].astype(jnp.float32)
            cvalue = lax.dynamic_index_in_dim(vis_heads[:, :, 1], group, 2, keepdims=False)[chosen].astype(jnp.float32)
            cscores = jnp.einsum("jtd,jvd->jtv", cquery, ckey) * scale
            ctop = jnp.max(cscores, axis=2, keepdims=True)
            cweights = jnp.exp(cscores - ctop)
            ctotal = jnp.sum(cweights, axis=2, keepdims=True)
            cnum = jnp.einsum("jtv,jvd->jtd", cweights.astype(jnp.bfloat16).astype(jnp.float32), cvalue)
            cross_ctx = (cnum / ctotal).astype(jnp.bfloat16).reshape(length, HEAD_DIM)
            return self_ctx, cross_ctx

        self_all, cross_all = lax.map(one_head, jnp.arange(HEADS, dtype=jnp.int32))
        mixed = self_all.astype(jnp.float32) + gate * cross_all.astype(jnp.float32)
        return mixed.transpose(1, 0, 2).reshape(length, HEADS * HEAD_DIM).astype(jnp.bfloat16)

    return lax.map(one_doc, (self_q, self_kv, doc_ids, cross_q, vision_kv, span_image, image_slot))
```

```python
import math

import jax
import jax.numpy as jnp
from jax import lax
from jax.experimental import pallas as pl
from jax.experimental.pallas import tpu as pltpu
from jax.sharding import Mesh, PartitionSpec as P

HEADS = 32
KV_HEADS = 8
DIM = 128
GROUP = HEADS // KV_HEADS
HOPS = 4
ID_ROWS = 16
VMEM = 62 * 2**20
NEG = -1e30
EXP2_SCALE = DIM ** -0.5 * math.log2(math.e)

ROWS, LINE, CORES = 2, 8, 2
AXES = ("zh", "y", "core", "x", "zl")
SEQ = ("zh", "y", "core")
DOC = ("x", "zl")


def place(zh, y, core):
    return (zh * LINE + y) * CORES + core


def pairs(moves):
    return [(place(*a, c), place(*b, c)) for a, b in moves for c in range(CORES)]


SWAP = [(place(z, y, c), place(z, y, 1 - c)) for z in range(ROWS) for y in range(LINE) for c in range(CORES)]


CROSS = pairs([((0, LINE - HOPS + j), (1, j)) for j in range(HOPS)])
LAST = pairs([((0, LINE - 1), (1, 0))])


def back_step(step):
    return pairs([((1, j + 1), (1, j)) for j in range(HOPS - step)])


def move(value, perm):
    return lax.ppermute(value, SEQ, perm)


def self_kernel(place_ref, q_own_ref, q_far_ref, *refs):
    count = 2 * HOPS + 1
    keys, values, ids = refs[:count], refs[count : 2 * count], refs[2 * count : 3 * count]
    out_own_ref, out_far_ref, bias_ref = refs[3 * count :]
    span = keys[0].shape[0]
    row, y, core = place_ref[0], place_ref[1], place_ref[2]

    def window(parts, take):
        blocks = [take(parts[0][...])]
        for hop in range(1, HOPS + 1):
            blocks.append(jnp.where(y >= hop, take(parts[hop][0]), take(parts[HOPS + hop][...])))
        return blocks

    @pl.when(pl.program_id(0) == 0)
    def _():
        numbers = window(ids, lambda block: jnp.broadcast_to(block[0:1].astype(jnp.float32), (span, span)))
        of_query = numbers[0].T
        own_half = core * (span // CORES)
        q_at = lax.broadcasted_iota(jnp.int32, (span, span), 0) ^ own_half
        k_at = lax.broadcasted_iota(jnp.int32, (span, span), 1) ^ own_half
        for hop in range(HOPS + 1):
            seen = numbers[hop] == of_query
            if hop == 0:
                seen = seen & (k_at <= q_at)
            else:
                seen = seen & ((row > 0) | (y >= hop))
            bias_ref[:, hop * span : (hop + 1) * span] = jnp.where(seen, 0.0, NEG)

    key = jnp.concatenate(window(keys, lambda block: block), 0)
    value = jnp.concatenate(window(values, lambda block: block), 0)
    rows = q_own_ref.shape[0]
    for h in range(GROUP):
        cols = slice(h * DIM, (h + 1) * DIM)
        query = jnp.concatenate([q_own_ref[:, cols], q_far_ref[:, cols]], 0)
        s = lax.dot_general(query, key, (((1,), (1,)), ((), ())), preferred_element_type=jnp.float32)
        s = s + bias_ref[...]
        top = jnp.max(s, axis=1, keepdims=True)
        w = jnp.exp2((s - top) * EXP2_SCALE)
        den = jnp.sum(w, axis=1, keepdims=True)
        num = jnp.dot(w.astype(jnp.bfloat16), value, preferred_element_type=jnp.float32)
        ctx = (num / den).astype(jnp.bfloat16)
        out_own_ref[:, cols] = ctx[:rows]
        out_far_ref[:, cols] = ctx[rows:]


def self_attention(place, q_own, q_far, own, line, across):
    tokens, width = q_own.shape
    span = CORES * tokens
    half = KV_HEADS // CORES
    window = (HOPS + 1) * span
    q_spec = pl.BlockSpec((tokens, GROUP * DIM), lambda g, at: (0, g))

    def specs(shape, index):
        before = [lambda g, at, hop=hop: (jnp.maximum(at[1] - hop, 0),) + index(g) for hop in range(1, HOPS + 1)]
        plain = pl.BlockSpec(shape, lambda g, at: index(g))
        return [plain] + [pl.BlockSpec((1,) + shape, f) for f in before] + [plain] * HOPS

    return pl.pallas_call(
        self_kernel,
        grid_spec=pltpu.PrefetchScalarGridSpec(
            num_scalar_prefetch=1,
            grid=(half,),
            in_specs=[q_spec, q_spec]
            + specs((span, DIM), lambda g: (0, g))
            + specs((span, DIM), lambda g: (0, half + g))
            + specs((ID_ROWS, span), lambda g: (span // ID_ROWS, 0)),
            out_specs=[q_spec, q_spec],
            scratch_shapes=[pltpu.VMEM((span, window), jnp.float32)],
        ),
        out_shape=[jax.ShapeDtypeStruct((tokens, width), jnp.bfloat16)] * 2,
        compiler_params=pltpu.CompilerParams(vmem_limit_bytes=VMEM),
        cost_estimate=pl.CostEstimate(
            flops=4 * span * window * width, bytes_accessed=8 * 2**20, transcendentals=span * window * width // DIM
        ),
        name="self_attention",
    )(place, q_own, q_far, *([own] + [line] * HOPS + across) * 3)


def pick_kernel(rows_ref, places_ref, table_ref, out_ref):
    for i in range(out_ref.shape[0]):
        out_ref[i] = table_ref[rows_ref[i], :, places_ref[i]]


def pick(slots, table):
    places = table.shape[2]
    smem, vmem = pl.BlockSpec(memory_space=pltpu.SMEM), pl.BlockSpec(memory_space=pltpu.VMEM)
    return pl.pallas_call(
        pick_kernel,
        in_specs=[smem, smem, vmem],
        out_specs=vmem,
        out_shape=jax.ShapeDtypeStruct(slots.shape + (table.shape[1],) + table.shape[3:], table.dtype),
        cost_estimate=pl.CostEstimate(flops=0, bytes_accessed=4 * table.size, transcendentals=0),
        compiler_params=pltpu.CompilerParams(vmem_limit_bytes=VMEM),
        name="pick_images",
    )(slots // places, slots % places, table)


def cross_kernel(core_ref, gate_ref, q_ref, key_ref, value_ref, own_ref, far_ref, out_ref):
    here = (pl.program_id(0) // (KV_HEADS // CORES)) == core_ref[0]
    gate = gate_ref[0]
    spans = key_ref.shape[1]
    span = q_ref.shape[0] // spans
    for j in range(spans):
        rows = slice(j * span, (j + 1) * span)
        q = jnp.concatenate([q_ref[rows, h * DIM : (h + 1) * DIM] for h in range(GROUP)], 0)
        s = lax.dot_general(q, key_ref[0, j], (((1,), (1,)), ((), ())), preferred_element_type=jnp.float32)
        top = jnp.max(s, axis=1, keepdims=True)
        w = jnp.exp2((s - top) * EXP2_SCALE)
        den = jnp.sum(w, axis=1, keepdims=True)
        num = jnp.dot(w.astype(jnp.bfloat16), value_ref[0, j], preferred_element_type=jnp.float32)
        cross = (num / den).astype(jnp.bfloat16).astype(jnp.float32)
        for h in range(GROUP):
            cols = slice(h * DIM, (h + 1) * DIM)
            own, far = own_ref[rows, cols].astype(jnp.float32), far_ref[rows, cols].astype(jnp.float32)
            mixed = jnp.where(here, own, far) + gate * cross[h * span : (h + 1) * span]
            out_ref[rows, cols] = mixed.astype(jnp.bfloat16)


def cross_attention(core, gate, cross_q, images, own, far):
    tokens, width = cross_q.shape
    half = KV_HEADS // CORES
    smem = pl.BlockSpec(memory_space=pltpu.SMEM)
    q_spec = pl.BlockSpec((tokens, GROUP * DIM), lambda g: (0, g))
    half_spec = pl.BlockSpec((tokens, GROUP * DIM), lambda g: (0, g % half))
    image = (1,) + images.shape[1:]
    return pl.pallas_call(
        cross_kernel,
        grid=(KV_HEADS,),
        in_specs=[
            smem,
            smem,
            q_spec,
            pl.BlockSpec(image, lambda g: (g, 0, 0, 0)),
            pl.BlockSpec(image, lambda g: (KV_HEADS + g, 0, 0, 0)),
            half_spec,
            half_spec,
        ],
        out_specs=q_spec,
        out_shape=jax.ShapeDtypeStruct((tokens, width), jnp.bfloat16),
        cost_estimate=pl.CostEstimate(
            flops=4 * tokens * images.shape[2] * width,
            bytes_accessed=6 * 2**20,
            transcendentals=tokens * images.shape[2] * HEADS,
        ),
        compiler_params=pltpu.CompilerParams(vmem_limit_bytes=VMEM),
        name="cross_attention",
    )(core, gate, cross_q, images, images, own, far)


def on_device(self_q, self_kv, doc_ids, cross_q, vision_kv, span_image, image_slot, cross_gate):
    q, kv, cq = self_q[0], self_kv[0], cross_q[0]
    tokens = q.shape[0]
    core = lax.axis_index("core")
    first = core == 0

    def halves(value):
        lo, hi = jnp.split(value, 2, axis=1)
        return jnp.where(first, lo, hi), jnp.where(first, hi, lo)

    k_mine, k_other = halves(kv[:, : KV_HEADS * DIM])
    v_mine, v_other = halves(kv[:, KV_HEADS * DIM :])
    numbers = (doc_ids + 1).astype(jnp.bfloat16)
    width = KV_HEADS * DIM
    numbers_own = jnp.pad(numbers, ((0, ID_ROWS - 1), (0, width - tokens)))
    numbers_far = jnp.pad(numbers, ((0, ID_ROWS - 1), (tokens, width - 2 * tokens)))
    far = move(jnp.concatenate([jnp.concatenate([k_other, v_other], 1), numbers_far], 0), SWAP)
    own = jnp.concatenate([jnp.concatenate([k_mine, v_mine], 1), far[:tokens], numbers_own + far[tokens:]], 0)

    docs, chunk = vision_kv.shape[0], vision_kv.shape[2]
    places = LINE * CORES
    image = vision_kv[:, 0].reshape(docs, chunk, places, DIM).transpose(2, 0, 1, 3)
    spread = lax.all_to_all(image, ("y", "core"), 0, 0, tiled=True)

    back0 = move(own, CROSS)
    last = move(own, LAST)
    gathered, spread = lax.optimization_barrier((own, spread))
    line = lax.all_gather(gathered, "y", axis=0)
    spread = spread.transpose(1, 0, 2, 3)
    table = lax.all_to_all(jnp.concatenate([spread, spread], 0), ("zh",) + DOC, 0, 0, tiled=True)
    table = table.reshape(ROWS, docs, places, chunk, DIM)
    back1 = move(back0, back_step(1))
    back2 = move(back1, back_step(2))
    q_own, q_other = halves(q)
    q_far = move(q_other, SWAP)
    image_range = jnp.arange(image_slot.shape[1], dtype=jnp.int32)
    slot = jnp.sum(jnp.where(span_image[0][:, None] == image_range[None, :], image_slot[0][None, :], 0), axis=1)
    here = slot.reshape(ROWS, -1)
    here = jnp.where(lax.axis_index("zh") == 0, here[0], here[1])
    table, _, _ = lax.optimization_barrier((table, back2, last))
    chosen = pick(here, table)
    chosen = chosen.reshape((places, -1) + chosen.shape[1:])
    images = lax.all_to_all(chosen, ("y", "core"), 0, 0, tiled=True)
    images = images.reshape(images.shape[:2] + (-1, DIM))

    place = jnp.stack([lax.axis_index("zh"), lax.axis_index("y"), core]).astype(jnp.int32)
    ctx_own, ctx_other = self_attention(place, q_own, q_far, own, line, [last, back2, back1, back0])
    ctx_far = move(ctx_other, SWAP)
    mixed = cross_attention(place[2:], jnp.tanh(cross_gate), cq, images, ctx_own, ctx_far)
    return mixed[None]


def solution(mesh):
    split = Mesh(mesh.devices.reshape(ROWS, LINE, CORES, 4, 4), AXES)
    in_specs = (
        P(DOC, SEQ, None),
        P(DOC, SEQ, None),
        P(DOC, SEQ),
        P(DOC, SEQ, None),
        P(None, SEQ, DOC, None),
        P(DOC, None),
        P(DOC, None),
        P(),
    )
    return jax.shard_map(on_device, mesh=split, in_specs=in_specs, out_specs=P(DOC, SEQ, None), check_vma=False)
```

```python
import math

import jax
import jax.numpy as jnp
from jax import lax
from jax.experimental import pallas as pl
from jax.experimental.pallas import tpu as pltpu
from jax.sharding import Mesh, PartitionSpec as P

HEADS = 32
KV_HEADS = 8
DIM = 128
GROUP = HEADS // KV_HEADS
HOPS = 4
ID_ROWS = 16
VMEM = 62 * 2**20
NEG = -1e30
EXP2_SCALE = DIM ** -0.5 * math.log2(math.e)

ROWS, LINE, CORES = 2, 8, 2
AXES = ("zh", "y", "core", "x", "zl")
SEQ = ("zh", "y", "core")
DOC = ("x", "zl")


def place(zh, y, core):
    return (zh * LINE + y) * CORES + core


def pairs(moves):
    return [(place(*a, c), place(*b, c)) for a, b in moves for c in range(CORES)]


SWAP = [(place(z, y, c), place(z, y, 1 - c)) for z in range(ROWS) for y in range(LINE) for c in range(CORES)]


CROSS = pairs([((0, LINE - HOPS + j), (1, j)) for j in range(HOPS)])
LAST = pairs([((0, LINE - 1), (1, 0))])


def back_step(step):
    return pairs([((1, j + 1), (1, j)) for j in range(HOPS - step)])


def move(value, perm):
    return lax.ppermute(value, SEQ, perm)


def self_kernel(place_ref, q_own_ref, q_far_ref, *refs):
    count = 2 * HOPS + 1
    keys, values, ids = refs[:count], refs[count : 2 * count], refs[2 * count : 3 * count]
    out_own_ref, out_far_ref, bias_ref = refs[3 * count :]
    span = keys[0].shape[0]
    row, y, core = place_ref[0], place_ref[1], place_ref[2]

    def window(parts, take):
        blocks = [take(parts[0][...])]
        for hop in range(1, HOPS + 1):
            blocks.append(jnp.where(y >= hop, take(parts[hop][0]), take(parts[HOPS + hop][...])))
        return blocks

    @pl.when(pl.program_id(0) == 0)
    def _():
        numbers = window(ids, lambda block: jnp.broadcast_to(block[0:1].astype(jnp.float32), (span, span)))
        of_query = numbers[0].T
        own_half = core * (span // CORES)
        q_at = lax.broadcasted_iota(jnp.int32, (span, span), 0) ^ own_half
        k_at = lax.broadcasted_iota(jnp.int32, (span, span), 1) ^ own_half
        for hop in range(HOPS + 1):
            seen = numbers[hop] == of_query
            if hop == 0:
                seen = seen & (k_at <= q_at)
            else:
                seen = seen & ((row > 0) | (y >= hop))
            bias_ref[:, hop * span : (hop + 1) * span] = jnp.where(seen, 0.0, NEG)

    key = jnp.concatenate(window(keys, lambda block: block), 0)
    value = jnp.concatenate(window(values, lambda block: block), 0)
    value = jnp.concatenate([value, jnp.ones_like(value)], 1)
    rows = q_own_ref.shape[0]
    for h in range(GROUP):
        cols = slice(h * DIM, (h + 1) * DIM)
        for part, (q_ref, out_ref) in enumerate(((q_own_ref, out_own_ref), (q_far_ref, out_far_ref))):
            s = lax.dot_general(q_ref[:, cols], key, (((1,), (1,)), ((), ())), preferred_element_type=jnp.float32)
            s = s + bias_ref[part * rows : (part + 1) * rows, :]
            top = jnp.max(s, axis=1, keepdims=True)
            w = jnp.exp2((s - top) * EXP2_SCALE).astype(jnp.bfloat16)
            num = jnp.dot(w, value, preferred_element_type=jnp.float32)
            out_ref[:, cols] = (num[:, :DIM] / num[:, DIM:]).astype(jnp.bfloat16)


def self_attention(place, q_own, q_far, own, line, across):
    tokens, width = q_own.shape
    span = CORES * tokens
    half = KV_HEADS // CORES
    window = (HOPS + 1) * span
    q_spec = pl.BlockSpec((tokens, GROUP * DIM), lambda g, at: (0, g))

    def specs(shape, index):
        before = [lambda g, at, hop=hop: (jnp.maximum(at[1] - hop, 0),) + index(g) for hop in range(1, HOPS + 1)]
        plain = pl.BlockSpec(shape, lambda g, at: index(g))
        return [plain] + [pl.BlockSpec((1,) + shape, f) for f in before] + [plain] * HOPS

    return pl.pallas_call(
        self_kernel,
        grid_spec=pltpu.PrefetchScalarGridSpec(
            num_scalar_prefetch=1,
            grid=(half,),
            in_specs=[q_spec, q_spec]
            + specs((span, DIM), lambda g: (0, g))
            + specs((span, DIM), lambda g: (0, half + g))
            + specs((ID_ROWS, span), lambda g: (span // ID_ROWS, 0)),
            out_specs=[q_spec, q_spec],
            scratch_shapes=[pltpu.VMEM((span, window), jnp.float32)],
        ),
        out_shape=[jax.ShapeDtypeStruct((tokens, width), jnp.bfloat16)] * 2,
        compiler_params=pltpu.CompilerParams(vmem_limit_bytes=VMEM),
        cost_estimate=pl.CostEstimate(
            flops=4 * span * window * width, bytes_accessed=8 * 2**20, transcendentals=span * window * width // DIM
        ),
        name="self_attention",
    )(place, q_own, q_far, *([own] + [line] * HOPS + across) * 3)


def pick_kernel(rows_ref, places_ref, table_ref, out_ref):
    for i in range(out_ref.shape[0]):
        out_ref[i] = table_ref[rows_ref[i], :, places_ref[i]]


def pick(slots, table):
    places = table.shape[2]
    smem, vmem = pl.BlockSpec(memory_space=pltpu.SMEM), pl.BlockSpec(memory_space=pltpu.VMEM)
    return pl.pallas_call(
        pick_kernel,
        in_specs=[smem, smem, vmem],
        out_specs=vmem,
        out_shape=jax.ShapeDtypeStruct(slots.shape + (table.shape[1],) + table.shape[3:], table.dtype),
        cost_estimate=pl.CostEstimate(flops=0, bytes_accessed=4 * table.size, transcendentals=0),
        compiler_params=pltpu.CompilerParams(vmem_limit_bytes=VMEM),
        name="pick_images",
    )(slots // places, slots % places, table)


def cross_kernel(core_ref, gate_ref, q_ref, key_ref, value_ref, own_ref, far_ref, out_ref):
    here = pl.program_id(0) == core_ref[0]
    gate = gate_ref[0]
    heads, spans = key_ref.shape[:2]
    span = q_ref.shape[0] // spans
    for g in range(heads):
        for j in range(spans):
            rows = slice(j * span, (j + 1) * span)
            places = [slice((g * GROUP + h) * DIM, (g * GROUP + h + 1) * DIM) for h in range(GROUP)]
            q = jnp.concatenate([q_ref[rows, cols] for cols in places], 0)
            s = lax.dot_general(q, key_ref[g, j], (((1,), (1,)), ((), ())), preferred_element_type=jnp.float32)
            top = jnp.max(s, axis=1, keepdims=True)
            w = jnp.exp2((s - top) * EXP2_SCALE)
            den = jnp.sum(w, axis=1, keepdims=True)
            num = jnp.dot(w.astype(jnp.bfloat16), value_ref[g, j], preferred_element_type=jnp.float32)
            cross = (num / den).astype(jnp.bfloat16).astype(jnp.float32)
            for h, cols in enumerate(places):
                own, far = own_ref[rows, cols].astype(jnp.float32), far_ref[rows, cols].astype(jnp.float32)
                mixed = jnp.where(here, own, far) + gate * cross[h * span : (h + 1) * span]
                out_ref[rows, cols] = mixed.astype(jnp.bfloat16)


def cross_attention(core, gate, cross_q, images, own, far):
    tokens, width = cross_q.shape
    half = KV_HEADS // CORES
    smem = pl.BlockSpec(memory_space=pltpu.SMEM)
    q_spec = pl.BlockSpec((tokens, width // CORES), lambda c: (0, c))
    half_spec = pl.BlockSpec((tokens, width // CORES), lambda c: (0, 0))
    image = (half,) + images.shape[1:]
    return pl.pallas_call(
        cross_kernel,
        grid=(CORES,),
        in_specs=[
            smem,
            smem,
            q_spec,
            pl.BlockSpec(image, lambda c: (c, 0, 0, 0)),
            pl.BlockSpec(image, lambda c: (CORES + c, 0, 0, 0)),
            half_spec,
            half_spec,
        ],
        out_specs=q_spec,
        out_shape=jax.ShapeDtypeStruct((tokens, width), jnp.bfloat16),
        cost_estimate=pl.CostEstimate(
            flops=4 * tokens * images.shape[2] * width,
            bytes_accessed=6 * 2**20,
            transcendentals=tokens * images.shape[2] * HEADS,
        ),
        compiler_params=pltpu.CompilerParams(vmem_limit_bytes=VMEM),
        name="cross_attention",
    )(core, gate, cross_q, images, images, own, far)


def on_device(self_q, self_kv, doc_ids, cross_q, vision_kv, span_image, image_slot, cross_gate):
    q, kv, cq = self_q[0], self_kv[0], cross_q[0]
    tokens = q.shape[0]
    core = lax.axis_index("core")
    first = core == 0

    def halves(value):
        lo, hi = jnp.split(value, 2, axis=1)
        return jnp.where(first, lo, hi), jnp.where(first, hi, lo)

    k_mine, k_other = halves(kv[:, : KV_HEADS * DIM])
    v_mine, v_other = halves(kv[:, KV_HEADS * DIM :])
    numbers = (doc_ids + 1).astype(jnp.bfloat16)
    width = KV_HEADS * DIM
    numbers_own = jnp.pad(numbers, ((0, ID_ROWS - 1), (0, width - tokens)))
    numbers_far = jnp.pad(numbers, ((0, ID_ROWS - 1), (tokens, width - 2 * tokens)))
    far = move(jnp.concatenate([jnp.concatenate([k_other, v_other], 1), numbers_far], 0), SWAP)
    own = jnp.concatenate([jnp.concatenate([k_mine, v_mine], 1), far[:tokens], numbers_own + far[tokens:]], 0)

    docs, chunk = vision_kv.shape[0], vision_kv.shape[2]
    places = LINE * CORES
    image = vision_kv[:, 0].reshape(docs, chunk, places, DIM).transpose(2, 0, 1, 3)
    spread = lax.all_to_all(image, ("y", "core"), 0, 0, tiled=True)

    back0 = move(own, CROSS)
    last = move(own, LAST)
    gathered, spread = lax.optimization_barrier((own, spread))
    line = lax.all_gather(gathered, "y", axis=0)
    spread = spread.transpose(1, 0, 2, 3)
    table = lax.all_to_all(jnp.concatenate([spread, spread], 0), ("zh",) + DOC, 0, 0, tiled=True)
    table = table.reshape(ROWS, docs, places, chunk, DIM)
    back1 = move(back0, back_step(1))
    back2 = move(back1, back_step(2))
    q_own, q_other = halves(q)
    q_far = move(q_other, SWAP)
    image_range = jnp.arange(image_slot.shape[1], dtype=jnp.int32)
    slot = jnp.sum(jnp.where(span_image[0][:, None] == image_range[None, :], image_slot[0][None, :], 0), axis=1)
    here = slot.reshape(ROWS, -1)
    here = jnp.where(lax.axis_index("zh") == 0, here[0], here[1])
    table, _, _ = lax.optimization_barrier((table, back2, last))
    chosen = pick(here, table)
    chosen = chosen.reshape((places, -1) + chosen.shape[1:])
    images = lax.all_to_all(chosen, ("y", "core"), 0, 0, tiled=True)
    images = images.reshape(images.shape[:2] + (-1, DIM))

    place = jnp.stack([lax.axis_index("zh"), lax.axis_index("y"), core]).astype(jnp.int32)
    ctx_own, ctx_other = self_attention(place, q_own, q_far, own, line, [last, back2, back1, back0])
    ctx_far = move(ctx_other, SWAP)
    mixed = cross_attention(place[2:], jnp.tanh(cross_gate), cq, images, ctx_own, ctx_far)
    return mixed[None]


def solution(mesh):
    split = Mesh(mesh.devices.reshape(ROWS, LINE, CORES, 4, 4), AXES)
    in_specs = (
        P(DOC, SEQ, None),
        P(DOC, SEQ, None),
        P(DOC, SEQ),
        P(DOC, SEQ, None),
        P(None, SEQ, DOC, None),
        P(DOC, None),
        P(DOC, None),
        P(),
    )
    return jax.shard_map(on_device, mesh=split, in_specs=in_specs, out_specs=P(DOC, SEQ, None), check_vma=False)
```

```python
import functools
import math

import jax
import jax.numpy as jnp
from jax import lax
from jax.experimental import pallas as pl
from jax.experimental.pallas import tpu as pltpu
from jax.sharding import Mesh, PartitionSpec as P

HEADS = 32
KV_HEADS = 8
DIM = 128
GROUP = HEADS // KV_HEADS
HOPS = 4
ID_ROWS = 16
VMEM = 62 * 2**20
NEG = -1e30
EXP2_SCALE = DIM ** -0.5 * math.log2(math.e)

ROWS, LINE, CORES = 2, 8, 2
AXES = ("zh", "y", "core", "x", "zl")
SEQ = ("zh", "y", "core")
DOC = ("x", "zl")


def place(zh, y, core):
    return (zh * LINE + y) * CORES + core


def pairs(moves):
    return [(place(*a, c), place(*b, c)) for a, b in moves for c in range(CORES)]


SWAP = [(place(z, y, c), place(z, y, 1 - c)) for z in range(ROWS) for y in range(LINE) for c in range(CORES)]


CROSS = pairs([((0, LINE - HOPS + j), (1, j)) for j in range(HOPS)])
LAST = pairs([((0, LINE - 1), (1, 0))])


def back_step(step):
    return pairs([((1, j + 1), (1, j)) for j in range(HOPS - step)])


def move(value, perm):
    return lax.ppermute(value, SEQ, perm)


def self_kernel(part, place_ref, q_ref, *refs):
    count = 2 * HOPS + 1
    keys, values, ids = refs[:count], refs[count : 2 * count], refs[2 * count : 3 * count]
    out_ref, bias_ref = refs[3 * count :]
    tokens = q_ref.shape[0]
    rows = slice(part * tokens, (part + 1) * tokens)
    span = keys[0].shape[0]
    row, y, core = place_ref[0], place_ref[1], place_ref[2]

    def window(parts, take):
        blocks = [take(parts[0][...])]
        for hop in range(1, HOPS + 1):
            blocks.append(jnp.where(y >= hop, take(parts[hop][0]), take(parts[HOPS + hop][...])))
        return blocks

    @pl.when(pl.program_id(0) == 0)
    def _():
        numbers = window(ids, lambda block: jnp.broadcast_to(block[0:1].astype(jnp.float32), (span, span)))
        of_query = numbers[0].T[rows]
        numbers = [number[:tokens] for number in numbers]
        own_half = core * (span // CORES)
        q_at = (lax.broadcasted_iota(jnp.int32, (tokens, span), 0) + part * tokens) ^ own_half
        k_at = lax.broadcasted_iota(jnp.int32, (tokens, span), 1) ^ own_half
        for hop in range(HOPS + 1):
            seen = numbers[hop] == of_query
            if hop == 0:
                seen = seen & (k_at <= q_at)
            else:
                seen = seen & ((row > 0) | (y >= hop))
            bias_ref[:, hop * span : (hop + 1) * span] = jnp.where(seen, 0.0, NEG)

    key = jnp.concatenate(window(keys, lambda block: block), 0)
    value = jnp.concatenate(window(values, lambda block: block), 0)
    value = jnp.concatenate([value, jnp.ones_like(value)], 1)
    for h in range(GROUP):
        cols = slice(h * DIM, (h + 1) * DIM)
        s = lax.dot_general(q_ref[:, cols], key, (((1,), (1,)), ((), ())), preferred_element_type=jnp.float32)
        s = s + bias_ref[...]
        top = jnp.max(s, axis=1, keepdims=True)
        w = jnp.exp2((s - top) * EXP2_SCALE).astype(jnp.bfloat16)
        num = jnp.dot(w, value, preferred_element_type=jnp.float32)
        out_ref[:, cols] = (num[:, :DIM] / num[:, DIM:]).astype(jnp.bfloat16)


def self_attention(part, place, q, own, line, across):
    tokens, width = q.shape
    span = CORES * tokens
    half = KV_HEADS // CORES
    window = (HOPS + 1) * span
    q_spec = pl.BlockSpec((tokens, GROUP * DIM), lambda g, at: (0, g))

    def specs(shape, index):
        before = [lambda g, at, hop=hop: (jnp.maximum(at[1] - hop, 0),) + index(g) for hop in range(1, HOPS + 1)]
        plain = pl.BlockSpec(shape, lambda g, at: index(g))
        return [plain] + [pl.BlockSpec((1,) + shape, f) for f in before] + [plain] * HOPS

    return pl.pallas_call(
        functools.partial(self_kernel, part),
        grid_spec=pltpu.PrefetchScalarGridSpec(
            num_scalar_prefetch=1,
            grid=(half,),
            in_specs=[q_spec]
            + specs((span, DIM), lambda g: (0, g))
            + specs((span, DIM), lambda g: (0, half + g))
            + specs((ID_ROWS, span), lambda g: (span // ID_ROWS, 0)),
            out_specs=q_spec,
            scratch_shapes=[pltpu.VMEM((tokens, window), jnp.float32)],
        ),
        out_shape=jax.ShapeDtypeStruct((tokens, width), jnp.bfloat16),
        compiler_params=pltpu.CompilerParams(vmem_limit_bytes=VMEM),
        cost_estimate=pl.CostEstimate(
            flops=4 * tokens * window * width, bytes_accessed=8 * 2**20, transcendentals=tokens * window * width // DIM
        ),
        name="self_attention",
    )(place, q, *([own] + [line] * HOPS + across) * 3)


def pick_kernel(rows_ref, places_ref, table_ref, out_ref):
    for i in range(out_ref.shape[0]):
        out_ref[i] = table_ref[rows_ref[i], :, places_ref[i]]


def pick(slots, table):
    places = table.shape[2]
    smem, vmem = pl.BlockSpec(memory_space=pltpu.SMEM), pl.BlockSpec(memory_space=pltpu.VMEM)
    return pl.pallas_call(
        pick_kernel,
        in_specs=[smem, smem, vmem],
        out_specs=vmem,
        out_shape=jax.ShapeDtypeStruct(slots.shape + (table.shape[1],) + table.shape[3:], table.dtype),
        cost_estimate=pl.CostEstimate(flops=0, bytes_accessed=4 * table.size, transcendentals=0),
        compiler_params=pltpu.CompilerParams(vmem_limit_bytes=VMEM),
        name="pick_images",
    )(slots // places, slots % places, table)


def cross_kernel(core_ref, gate_ref, q_ref, key_ref, value_ref, own_ref, far_ref, out_ref):
    here = pl.program_id(0) == core_ref[0]
    gate = gate_ref[0]
    heads, spans = key_ref.shape[:2]
    span = q_ref.shape[0] // spans
    for g in range(heads):
        for j in range(spans):
            rows = slice(j * span, (j + 1) * span)
            places = [slice((g * GROUP + h) * DIM, (g * GROUP + h + 1) * DIM) for h in range(GROUP)]
            q = jnp.concatenate([q_ref[rows, cols] for cols in places], 0)
            s = lax.dot_general(q, key_ref[g, j], (((1,), (1,)), ((), ())), preferred_element_type=jnp.float32)
            top = jnp.max(s, axis=1, keepdims=True)
            w = jnp.exp2((s - top) * EXP2_SCALE)
            den = jnp.sum(w, axis=1, keepdims=True)
            num = jnp.dot(w.astype(jnp.bfloat16), value_ref[g, j], preferred_element_type=jnp.float32)
            cross = (num / den).astype(jnp.bfloat16).astype(jnp.float32)
            for h, cols in enumerate(places):
                own, far = own_ref[rows, cols].astype(jnp.float32), far_ref[rows, cols].astype(jnp.float32)
                mixed = jnp.where(here, own, far) + gate * cross[h * span : (h + 1) * span]
                out_ref[rows, cols] = mixed.astype(jnp.bfloat16)


def cross_attention(core, gate, cross_q, images, own, far):
    tokens, width = cross_q.shape
    half = KV_HEADS // CORES
    smem = pl.BlockSpec(memory_space=pltpu.SMEM)
    q_spec = pl.BlockSpec((tokens, width // CORES), lambda c: (0, c))
    half_spec = pl.BlockSpec((tokens, width // CORES), lambda c: (0, 0))
    image = (half,) + images.shape[1:]
    return pl.pallas_call(
        cross_kernel,
        grid=(CORES,),
        in_specs=[
            smem,
            smem,
            q_spec,
            pl.BlockSpec(image, lambda c: (c, 0, 0, 0)),
            pl.BlockSpec(image, lambda c: (CORES + c, 0, 0, 0)),
            half_spec,
            half_spec,
        ],
        out_specs=q_spec,
        out_shape=jax.ShapeDtypeStruct((tokens, width), jnp.bfloat16),
        cost_estimate=pl.CostEstimate(
            flops=4 * tokens * images.shape[2] * width,
            bytes_accessed=6 * 2**20,
            transcendentals=tokens * images.shape[2] * HEADS,
        ),
        compiler_params=pltpu.CompilerParams(vmem_limit_bytes=VMEM),
        name="cross_attention",
    )(core, gate, cross_q, images, images, own, far)


def on_device(self_q, self_kv, doc_ids, cross_q, vision_kv, span_image, image_slot, cross_gate):
    q, kv, cq = self_q[0], self_kv[0], cross_q[0]
    tokens = q.shape[0]
    core = lax.axis_index("core")
    first = core == 0

    def halves(value):
        lo, hi = jnp.split(value, 2, axis=1)
        return jnp.where(first, lo, hi), jnp.where(first, hi, lo)

    k_mine, k_other = halves(kv[:, : KV_HEADS * DIM])
    v_mine, v_other = halves(kv[:, KV_HEADS * DIM :])
    numbers = (doc_ids + 1).astype(jnp.bfloat16)
    width = KV_HEADS * DIM
    numbers_own = jnp.pad(numbers, ((0, ID_ROWS - 1), (0, width - tokens)))
    numbers_far = jnp.pad(numbers, ((0, ID_ROWS - 1), (tokens, width - 2 * tokens)))
    far = move(jnp.concatenate([jnp.concatenate([k_other, v_other], 1), numbers_far], 0), SWAP)
    own = jnp.concatenate([jnp.concatenate([k_mine, v_mine], 1), far[:tokens], numbers_own + far[tokens:]], 0)

    docs, chunk = vision_kv.shape[0], vision_kv.shape[2]
    places = LINE * CORES
    image = vision_kv[:, 0].reshape(docs, chunk, places, DIM).transpose(2, 0, 1, 3)
    spread = lax.all_to_all(image, ("y", "core"), 0, 0, tiled=True)

    back0 = move(own, CROSS)
    last = move(own, LAST)
    gathered, spread = lax.optimization_barrier((own, spread))
    line = lax.all_gather(gathered, "y", axis=0)
    spread = spread.transpose(1, 0, 2, 3)
    table = lax.all_to_all(jnp.concatenate([spread, spread], 0), ("zh",) + DOC, 0, 0, tiled=True)
    table = table.reshape(ROWS, docs, places, chunk, DIM)
    back1 = move(back0, back_step(1))
    back2 = move(back1, back_step(2))
    q_own, q_other = halves(q)
    q_far = move(q_other, SWAP)
    image_range = jnp.arange(image_slot.shape[1], dtype=jnp.int32)
    slot = jnp.sum(jnp.where(span_image[0][:, None] == image_range[None, :], image_slot[0][None, :], 0), axis=1)
    here = slot.reshape(ROWS, -1)
    here = jnp.where(lax.axis_index("zh") == 0, here[0], here[1])
    table, _, _ = lax.optimization_barrier((table, back2, last))
    chosen = pick(here, table)
    chosen = chosen.reshape((places, -1) + chosen.shape[1:])
    images = lax.all_to_all(chosen, ("y", "core"), 0, 0, tiled=True)
    images = images.reshape(images.shape[:2] + (-1, DIM))

    place = jnp.stack([lax.axis_index("zh"), lax.axis_index("y"), core]).astype(jnp.int32)
    ctx_other = self_attention(1, place, q_far, own, line, [last, back2, back1, back0])
    ctx_own = self_attention(0, place, q_own, own, line, [last, back2, back1, back0])
    ctx_far = move(ctx_other, SWAP)
    mixed = cross_attention(place[2:], jnp.tanh(cross_gate), cq, images, ctx_own, ctx_far)
    return mixed[None]


def solution(mesh):
    split = Mesh(mesh.devices.reshape(ROWS, LINE, CORES, 4, 4), AXES)
    in_specs = (
        P(DOC, SEQ, None),
        P(DOC, SEQ, None),
        P(DOC, SEQ),
        P(DOC, SEQ, None),
        P(None, SEQ, DOC, None),
        P(DOC, None),
        P(DOC, None),
        P(),
    )
    return jax.shard_map(on_device, mesh=split, in_specs=in_specs, out_specs=P(DOC, SEQ, None), check_vma=False)
```
